512 devices in a mesh: ctx: 16 (over x, y_hi, core), tp: 32 (over y_lo, z).
Axes of the slice: x: 4, y: 8 (y_hi: 2, y_lo: 4; y = y_hi * 4 + y_lo), z: 8, core: 2. Of those that a mesh axis runs over, the one named last changes fastest.
Arguments:
- tokens: bfloat16 [8192, 8192], P('ctx', 'tp'), may hold values from -400 to 400
- norm_gain: bfloat16 [8192], P('tp'), may hold values from 0.099609375 to 1.8984375
- in_weight: bfloat16 [8192, 3, 8192], P('ctx', None, 'tp'), may hold values from -0.0625 to 0.0625
- short_weight: float32 [3, 3, 8192], P(None, None, 'tp'), may hold values from -3.5 to 3.5
- filters: bfloat16 [512, 128], P('tp'), may hold values from -0.5 to 0.5
Outputs:
- mixed: bfloat16 [8192, 8192], P('ctx', 'tp')
The draws below stay inside these ranges and needn't reach their ends.
All inputs are finite; a program needn't handle non-finite values.
Results may differ from the reference program's by a relative error of at most 0.0091.
Values may be sent and summed in bfloat16 or wider, within the bound.
A program may use at most 128 MiB of HBM per device.

```python
import jax
import jax.numpy as jnp
from jax import lax

D = 8192
GROUP = 16
TAPS = 128
SHORT = 3
TOKENS = 8192


def draw_tokens(key, part):
    first, second = jax.random.split(key, 2)
    columns = 10.0 ** (jnp.arange(D, dtype=jnp.float32) / D)
    values = jax.random.truncated_normal(first, -4.0, 4.0, (TOKENS, D), jnp.float32)
    rowscale = 10.0 ** jax.random.uniform(second, (TOKENS, 1), jnp.float32, 0.0, 1.0)
    return (values * rowscale * columns).astype(jnp.bfloat16)


def block_scale(own_key, shape, cuts, least, high):
    gain, own = 1.0, jax.random.fold_in(own_key, 6)
    for axis_at, parts in cuts:
        steps = jnp.exp(jax.random.uniform(jax.random.fold_in(own, axis_at), (parts,), jnp.float32, least / len(cuts), high / len(cuts)))
        gain = gain * jnp.repeat(steps, shape[axis_at] // parts).reshape([-1 if axis == axis_at else 1 for axis in range(len(shape))])
    return gain


def noise(stream_key, shape, spread, most, cuts=(), kind=jnp.bfloat16):
    entries = jax.random.normal(stream_key, shape, jnp.float32) * spread
    if len(cuts) > 0:
        entries = block_scale(stream_key, shape, cuts, -0.22, 0.18) * entries
    return jnp.clip(entries, min=-most, max=most).astype(kind)


def setup_inputs(seed: int = 0) -> dict:
    arg_keys = jax.random.split(jax.random.key(seed), 6)
    return {
        "tokens": draw_tokens(jax.random.fold_in(arg_keys[5], 71), 0),
        "norm_gain": jnp.clip(1.0 + 0.18 * jax.random.normal(arg_keys[1], (D,), jnp.float32), 0.099609375, 1.8984375).astype(jnp.bfloat16),
        "in_weight": noise(arg_keys[2], (D, 3, D), D ** -0.5, 0.0625, ((0, 16), (2, 32))),
        "short_weight": noise(arg_keys[3], (SHORT, 3, D), SHORT ** -0.5, 3.5, ((2, 32),), jnp.float32),
        "filters": noise(arg_keys[4], (D // GROUP, TAPS), TAPS ** -0.5, 0.5, ((0, 32),)),
    }


def toeplitz_pair(rows, taps):
    above = jnp.arange(taps)[:, None]
    across = jnp.arange(taps)[None, :]
    index = (across - above) % taps
    full = rows[:, index]
    zero = jnp.zeros((), rows.dtype)
    return (jnp.where(across >= above, full, zero), jnp.where(across < above, full, zero))

def reference(tokens, norm_gain, in_weight, short_weight, filters):
    count, width = tokens.shape
    xfull = tokens.astype(jnp.float32)
    scale = lax.rsqrt(lax.optimization_barrier(jnp.mean(xfull * xfull, axis=1, keepdims=True)) + 1e-06)
    normed = (xfull * scale * norm_gain.astype(jnp.float32)).astype(jnp.bfloat16)
    proj = jnp.dot(normed, in_weight.reshape(width, 3 * width), preferred_element_type=jnp.float32)
    proj = proj.reshape(count, 3, width).astype(jnp.bfloat16)
    padded = jnp.concatenate([jnp.zeros((SHORT - 1, 3, width), jnp.bfloat16), proj], 0).astype(jnp.float32)
    feat = jnp.zeros((count, 3, width), jnp.float32)
    for tap in range(SHORT):
        feat = feat + short_weight[tap].astype(jnp.float32) * padded[SHORT - 1 - tap:SHORT - 1 - tap + count]
    gated = (feat[:, 1] * feat[:, 2]).astype(jnp.bfloat16)
    groups = filters.shape[0]
    members = width // groups
    blocks = count // TAPS
    stack = gated.T.reshape(groups, members, blocks, TAPS)
    before = jnp.concatenate([jnp.zeros((groups, members, 1, TAPS), jnp.bfloat16), stack[:, :, :-1]], 2)
    near, far = toeplitz_pair(filters, TAPS)
    conv = jnp.einsum('gcbs,gsi->gcbi', stack.astype(jnp.float32), near.astype(jnp.float32))
    conv = conv + jnp.einsum('gcbs,gsi->gcbi', before.astype(jnp.float32), far.astype(jnp.float32))
    conv = conv.reshape(width, count).T.astype(jnp.bfloat16)
    return (feat[:, 0] * conv.astype(jnp.float32)).astype(jnp.bfloat16)
```

```python
import functools

import jax
import jax.numpy as jnp
from jax import lax
from jax.experimental import pallas as pl
from jax.experimental.pallas import tpu as pltpu
from jax.sharding import PartitionSpec as P

MESH = pl.DeviceIdType.MESH
F32 = jnp.float32
BF16 = jnp.bfloat16
ROWS = 512
COLS = 256
PIECES = 32
TAPS = 128
GROUP = 16
EXT = ROWS + 16
HALO = TAPS + 48


def kernel(
    tok_ref, gain_ref, w_ref, sw_ref, filt_ref, out_ref,
    a_buf, b_buf, xg, stage, acc, sq, toep, proj, gated, qbuf, wide, halo_out, halo_in,
    local_sem, send_sem, a_sem, b_sem, stage_sem, halo_sem,
):
    ctx = lax.axis_index("ctx")
    tp = lax.axis_index("tp")
    core = lax.rem(ctx, 2)
    yh = lax.rem(lax.div(ctx, 2), 2)
    x = lax.div(ctx, 4)
    z = lax.rem(tp, 8)
    yl = lax.div(tp, 8)
    y = yh * 4 + yl

    def at(dx=0, dy=0, dz=0):
        nx, ny, nz = lax.rem(x + dx + 4, 4), lax.rem(y + dy + 8, 8), lax.rem(z + dz + 8, 8)
        return ((nx * 2 + lax.div(ny, 4)) * 2 + core, lax.rem(ny, 4) * 8 + nz)

    lines = [yl, yl + 1 - 2 * lax.rem(yl, 2), lax.rem(yl + 2, 4), 3 - yl]
    line_dev = [(ctx, v * 8 + z) for v in lines]
    up, down = at(dz=1), at(dz=-1)
    east, west = at(dx=1), at(dx=-1)
    sibling = (ctx + 1 - 2 * core, tp)
    after, before = (lax.rem(ctx + 1, 16), tp), (lax.rem(ctx + 15, 16), tp)
    y1, ym1, y3, ym3 = at(dy=1), at(dy=-1), at(dy=3), at(dy=-3)

    sends = []

    def push(src, dst, sem, device):
        copy = pltpu.make_async_remote_copy(
            src_ref=src, dst_ref=dst, send_sem=send_sem.at[len(sends)], recv_sem=sem,
            device_id=device, device_id_type=MESH,
        )
        copy.start()
        sends.append(copy)

    def landed(slot, sem):
        pltpu.make_async_remote_copy(
            src_ref=slot, dst_ref=slot, send_sem=send_sem.at[0], recv_sem=sem,
            device_id=sibling, device_id_type=MESH,
        ).wait_recv()

    own = [
        pltpu.make_async_copy(tok_ref, a_buf.at[tp, pl.ds(0, ROWS)], local_sem.at[0]),
        pltpu.make_async_copy(gain_ref, a_buf.at[tp, pl.ds(ROWS, 16)], local_sem.at[1]),
    ]
    for h in range(2):
        own.append(
            pltpu.make_async_copy(
                w_ref.at[:, pl.ds(h * 256, 256)], b_buf.at[2 * ctx + h], local_sem.at[2 + h]
            )
        )
    for copy in own:
        copy.start()

    barrier = pltpu.get_barrier_semaphore()
    peers = [up, down, east, west, sibling, after, before, y1, ym1, y3, ym3] + line_dev[1:]
    for peer in peers:
        pl.semaphore_signal(barrier, inc=1, device_id=peer, device_id_type=MESH)
    for copy in own:
        copy.wait()
    pl.semaphore_wait(barrier, len(peers))

    def push_a(index, device):
        push(a_buf.at[index], a_buf.at[index], a_sem.at[index], device)

    def push_b(index, device):
        push(b_buf.at[index], b_buf.at[index], b_sem.at[index], device)

    def absorb(t):
        gain = a_buf[t, pl.ds(ROWS, 16), :][0:1].astype(F32)

        @pl.loop(0, ROWS // 64)
        def _(i):
            rows = pl.ds(pl.multiple_of(i * 64, 64), 64)
            values = a_buf[t, rows, :].astype(F32)
            square = values * values
            sq[rows, :] += square[:, :128] + square[:, 128:]
            xg[t, rows, :] = (values * gain).astype(BF16)

    def multiply(t):
        lhs = xg[t]
        for s in range(3):
            acc[s] += jnp.dot(lhs, b_buf[t, s], preferred_element_type=F32)

    mine = [2 * ctx, 2 * ctx + 1]
    push_a(tp, up)
    push_a(tp, down)
    push_b(mine[0], east)
    push_b(mine[1], west)
    push_a(tp, line_dev[1])
    push(b_buf.at[mine[0]], stage.at[0], stage_sem.at[0], y3)
    push(b_buf.at[mine[1]], stage.at[1], stage_sem.at[1], ym3)
    push_b(mine[1], east)
    push_b(mine[0], west)
    push_b(mine[0], sibling)
    push_b(mine[1], sibling)
    push_a(tp, line_dev[2])
    push_a(tp, line_dev[3])

    for s in range(3):
        acc[s] = jnp.zeros((ROWS, COLS), F32)
    sq[...] = jnp.zeros_like(sq)
    tap = lax.broadcasted_iota(jnp.int32, (TAPS, 2 * TAPS), 0)
    place = lax.broadcasted_iota(jnp.int32, (TAPS, 2 * TAPS), 1)
    flip = jnp.where(tap + place == TAPS, 1.0, 0.0).astype(BF16)
    flipped = jnp.dot(filt_ref[...], flip, preferred_element_type=F32)
    for g in range(GROUP):
        row = jnp.broadcast_to(flipped[g : g + 1, :], (TAPS, 2 * TAPS))
        toep[g * TAPS : (g + 1) * TAPS, :] = pltpu.roll(
            row, 0, 1, stride=1, stride_axis=0
        ).astype(BF16)
    absorb(tp)

    events = []
    slot_us, half_us = 5.3, 8.0

    def from_z(r, d, sign, last):
        def act():
            t = lines[r] * 8 + lax.rem(z - sign * d + 8, 8)
            landed(a_buf.at[t], a_sem.at[t])
            if d < last:
                push_a(t, up if sign > 0 else down)
            absorb(t)
        return act

    for sign in (1, -1):
        lasts = [4 if (r % 2 == 0) == (sign > 0) else 3 for r in range(4)]
        first = sorted([(d, r) for r in (0, 1) for d in range(1, lasts[r] + 1)])
        second = sorted([(d, r) for r in (2, 3) for d in range(1, lasts[r] + 1)])
        for k, (d, r) in enumerate(first + second):
            events.append(((k + 1) * slot_us, from_z(r, d, sign, lasts[r])))

    def from_line(r):
        def act():
            t = lines[r] * 8 + z
            landed(a_buf.at[t], a_sem.at[t])
            push_a(t, up)
            push_a(t, down)
            absorb(t)
        return act

    events.append((8.0, from_line(1)))
    events.append((30.0, from_line(2)))
    events.append((32.0, from_line(3)))

    def slot_of(dx, other, h):
        bx = lax.rem(x + dx + 4, 4)
        bh = (1 - yh) if other else yh
        return ((bx * 2 + bh) * 2 + core) * 2 + h

    def from_x(dx, other, h, onward):
        def act():
            t = slot_of(dx, other, h)
            landed(b_buf.at[t], b_sem.at[t])
            if onward is not None:
                push_b(t, onward)
            push_b(t, sibling)
        return act

    for other, base in ((False, 0.0), (True, 3 * half_us)):
        events.append((base + half_us + 0.1, from_x(-1, other, 0, east)))
        events.append((base + half_us + 0.2, from_x(1, other, 1, west)))
        events.append((base + 2 * half_us + 0.1, from_x(-1, other, 1, None)))
        events.append((base + 2 * half_us + 0.2, from_x(1, other, 0, None)))
        events.append((base + 3 * half_us + 0.1, from_x(2, other, 0, None)))
        events.append((base + 3 * half_us + 0.2, from_x(2, other, 1, None)))

    def crossing(h, leg):
        def act():
            if leg == 0:
                landed(stage.at[h], stage_sem.at[h])
                to = y1 if h == 0 else ym1
                origin = lax.rem(y - 3 + 8, 8) if h == 0 else lax.rem(y + 3, 8)
                t = ((x * 2 + lax.div(origin, 4)) * 2 + core) * 2 + h
                push(stage.at[h], b_buf.at[t], b_sem.at[t], to)
            else:
                t = slot_of(0, True, h)
                landed(b_buf.at[t], b_sem.at[t])
                push_b(t, east if h == 0 else west)
                push_b(t, west if h == 0 else east)
                push_b(t, sibling)
        return act

    events.append((15.5, crossing(0, 0)))
    events.append((15.6, crossing(1, 0)))
    events.append((23.0, crossing(0, 1)))
    events.append((23.1, crossing(1, 1)))

    def all_b():
        for k in range(16):
            t = (2 * lax.div(k, 2) + 1 - core) * 2 + (k % 2)
            landed(b_buf.at[t], b_sem.at[t])

        for r in (0, 1):
            @pl.loop(0, 8)
            def _(e):
                multiply(lines[r] * 8 + lax.rem(z + e, 8))

    events.append((56.0, all_b))
    for _, act in sorted(events, key=lambda event: event[0]):
        act()

    for r in (2, 3):
        @pl.loop(0, 8)
        def _(e):
            multiply(lines[r] * 8 + lax.rem(z + e, 8))

    head = proj.at[pl.ds(0, 16)]

    @pl.loop(0, ROWS // 128)
    def _(i):
        rows = pl.ds(pl.multiple_of(i * 128, 128), 128)
        total = jnp.sum(sq[rows, :], axis=1, keepdims=True)
        scale = lax.rsqrt(total / (PIECES * COLS) + 1e-06)
        for s in range(3):
            proj[pl.ds(pl.multiple_of(16 + i * 128, 16), 128), s * COLS : (s + 1) * COLS] = (
                acc[s, rows, :] * scale
            ).astype(BF16)

    def feat(b, s):
        lines_ = pl.ds(pl.multiple_of(b * 128, 16), 144)
        block = proj[lines_, s * COLS : (s + 1) * COLS].astype(F32)
        return (
            sw_ref[0, s : s + 1, :] * block[16:144]
            + sw_ref[1, s : s + 1, :] * block[15:143]
            + sw_ref[2, s : s + 1, :] * block[14:142]
        )

    def gate(b):
        gated[pl.ds(pl.multiple_of((b + 1) * 128, 128), 128), :] = (feat(b, 1) * feat(b, 2)).astype(BF16)

    def mix(b):
        window = gated[pl.ds(pl.multiple_of(b * 128, 128), 256), :]
        lane = lax.broadcasted_iota(jnp.int32, (TAPS, COLS), 1)
        conv = jnp.zeros((TAPS, COLS), F32)
        for g in range(GROUP):
            part = jnp.dot(
                toep[g * TAPS : (g + 1) * TAPS, :], window, preferred_element_type=F32
            )
            inside = (lane >= g * GROUP) & (lane < (g + 1) * GROUP)
            conv = jnp.where(inside, part, conv)
        conv = conv.astype(BF16).astype(F32)
        out_ref[pl.ds(pl.multiple_of(b * 128, 128), 128), :] = (feat(b, 0) * conv).astype(BF16)

    gate(3)
    halo_out[0:TAPS, :] = gated[512:640, :]
    for s in range(3):
        halo_out[TAPS + 16 * s : TAPS + 16 * (s + 1), :] = proj[512:528, s * COLS : (s + 1) * COLS]
    push(halo_out, halo_in, halo_sem.at[0], after)

    gate(1)
    gate(2)
    mix(2)
    mix(3)
    landed(halo_in, halo_sem.at[0])
    keep = jnp.where(ctx > 0, 1.0, 0.0).astype(BF16)
    gated[0:TAPS, :] = halo_in[0:TAPS, :] * keep
    for s in range(3):
        proj[0:16, s * COLS : (s + 1) * COLS] = halo_in[TAPS + 16 * s : TAPS + 16 * (s + 1), :] * keep
    gate(0)
    mix(0)
    mix(1)
    for copy in sends:
        copy.wait_send()


N_SENDS = 80


def per_device(tokens, norm_gain, in_weight, short_weight, filters):
    gains = jnp.broadcast_to(norm_gain[None, :], (16, COLS))
    weight = jnp.transpose(in_weight, (1, 0, 2))
    vmem = pl.BlockSpec(memory_space=pltpu.VMEM)
    hbm = pl.BlockSpec(memory_space=pl.ANY)
    return pl.pallas_call(
        kernel,
        out_shape=jax.ShapeDtypeStruct((ROWS, COLS), BF16),
        in_specs=[hbm, hbm, hbm, vmem, vmem],
        out_specs=vmem,
        scratch_shapes=[
            pltpu.VMEM((PIECES, EXT, COLS), BF16),
            pltpu.VMEM((PIECES, 3, 256, COLS), BF16),
            pltpu.VMEM((PIECES, ROWS, COLS), BF16),
            pltpu.VMEM((2, 3, 256, COLS), BF16),
            pltpu.VMEM((3, ROWS, COLS), F32),
            pltpu.VMEM((ROWS, 128), F32),
            pltpu.VMEM((GROUP * TAPS, 2 * TAPS), BF16),
            pltpu.VMEM((ROWS + 16, 3 * COLS), BF16),
            pltpu.VMEM((ROWS + TAPS, COLS), BF16),
            pltpu.VMEM((16, COLS), BF16),
            pltpu.VMEM((16, COLS), BF16),
            pltpu.VMEM((HALO, COLS), BF16),
            pltpu.VMEM((HALO, COLS), BF16),
            pltpu.SemaphoreType.DMA((4,)),
            pltpu.SemaphoreType.DMA((N_SENDS,)),
            pltpu.SemaphoreType.DMA((PIECES,)),
            pltpu.SemaphoreType.DMA((PIECES,)),
            pltpu.SemaphoreType.DMA((2,)),
            pltpu.SemaphoreType.DMA((1,)),
        ],
        compiler_params=pltpu.CompilerParams(
            collective_id=0, has_side_effects=True, vmem_limit_bytes=58 * 1024 * 1024
        ),
        cost_estimate=pl.CostEstimate(
            flops=2 * ROWS * 8192 * 768, bytes_accessed=4 * 1024 * 1024, transcendentals=0
        ),
    )(tokens, gains, weight, short_weight, filters)


def solution(mesh):
    placed = (P("ctx", "tp"), P("tp"), P("ctx", None, "tp"), P(None, None, "tp"), P("tp", None))
    return jax.shard_map(
        per_device, mesh=mesh, in_specs=placed, out_specs=P("ctx", "tp"), check_vma=False
    )
```

```python
import functools

import jax
import jax.numpy as jnp
from jax import lax
from jax.experimental import pallas as pl
from jax.experimental.pallas import tpu as pltpu
from jax.sharding import PartitionSpec as P

MESH = pl.DeviceIdType.MESH
F32 = jnp.float32
BF16 = jnp.bfloat16
ROWS = 512
COLS = 256
PIECES = 32
TAPS = 128
GROUP = 16
EXT = ROWS + 16
HALO = TAPS + 48


def kernel(
    tok_ref, gain_ref, w_ref, sw_ref, filt_ref, out_ref,
    a_buf, b_buf, xg, acc, sq, toep, proj, gated, halo_out, halo_in,
    local_sem, send_sem, a_sem, b_sem, halo_sem,
):
    ctx = lax.axis_index("ctx")
    tp = lax.axis_index("tp")
    core = lax.rem(ctx, 2)
    yh = lax.rem(lax.div(ctx, 2), 2)
    x = lax.div(ctx, 4)
    z = lax.rem(tp, 8)
    yl = lax.div(tp, 8)
    y = yh * 4 + yl

    def at(dx=0, dy=0, dz=0):
        nx, ny, nz = lax.rem(x + dx + 4, 4), lax.rem(y + dy + 8, 8), lax.rem(z + dz + 8, 8)
        return ((nx * 2 + lax.div(ny, 4)) * 2 + core, lax.rem(ny, 4) * 8 + nz)

    lines = [yl, yl + 1 - 2 * lax.rem(yl, 2), lax.rem(yl + 2, 4), 3 - yl]
    line_dev = [(ctx, v * 8 + z) for v in lines]
    up, down = at(dz=1), at(dz=-1)
    east, west = at(dx=1), at(dx=-1)
    sibling = (ctx + 1 - 2 * core, tp)
    after, before = (lax.rem(ctx + 1, 16), tp), (lax.rem(ctx + 15, 16), tp)
    across = at(dy=4)

    sends = []

    def push(src, dst, sem, device):
        copy = pltpu.make_async_remote_copy(
            src_ref=src, dst_ref=dst, send_sem=send_sem.at[len(sends)], recv_sem=sem,
            device_id=device, device_id_type=MESH,
        )
        copy.start()
        sends.append(copy)

    def landed(slot, sem):
        pltpu.make_async_remote_copy(
            src_ref=slot, dst_ref=slot, send_sem=send_sem.at[0], recv_sem=sem,
            device_id=sibling, device_id_type=MESH,
        ).wait_recv()

    own = [
        pltpu.make_async_copy(tok_ref, a_buf.at[tp, pl.ds(0, ROWS)], local_sem.at[0]),
    ]
    for s in range(3):
        columns = pl.ds(s * COLS, COLS)
        own.append(
            pltpu.make_async_copy(w_ref.at[s], b_buf.at[ctx, :, columns], local_sem.at[1 + s])
        )
    for copy in own:
        copy.start()
    a_buf[tp, pl.ds(ROWS, 16), :] = jnp.broadcast_to(gain_ref[...].reshape(1, COLS), (16, COLS))

    barrier = pltpu.get_barrier_semaphore()
    peers = [up, down, east, west, sibling, after, before, across] + line_dev[1:]
    for peer in peers:
        pl.semaphore_signal(barrier, inc=1, device_id=peer, device_id_type=MESH)
    for copy in own:
        copy.wait()
    pl.semaphore_wait(barrier, len(peers))

    def part(t, p):
        rows = pl.ds(0, ROWS // 2) if p == 0 else pl.ds(ROWS // 2, ROWS // 2 + 16)
        return a_buf.at[t, rows], a_sem.at[2 * t + p]

    def push_a(t, p, device):
        ref, sem = part(t, p)
        push(ref, ref, sem, device)

    def half(block, h):
        return b_buf.at[block, pl.ds(h * 256, 256)], b_sem.at[2 * block + h]

    def push_b(block, h, device):
        ref, sem = half(block, h)
        push(ref, ref, sem, device)

    def absorb(t):
        gain = a_buf[t, pl.ds(ROWS, 16), :][0:1].astype(F32)
        columns = pl.ds(pl.multiple_of(lax.rem(t, 2) * COLS, COLS), COLS)

        @pl.loop(0, ROWS // 64)
        def _(i):
            rows = pl.ds(pl.multiple_of(i * 64, 64), 64)
            values = a_buf[t, rows, :].astype(F32)
            square = values * values
            sq[rows, :] += square[:, :128] + square[:, 128:]
            xg[lax.div(t, 2), rows, columns] = (values * gain).astype(BF16)

    def multiply(block):
        @pl.loop(0, ROWS // MUL_ROWS)
        def _(i):
            rows = pl.ds(pl.multiple_of(i * MUL_ROWS, MUL_ROWS), MUL_ROWS)
            acc[rows, :] += jnp.dot(xg[block, rows, :], b_buf[block], preferred_element_type=F32)

    for p in range(2):
        push_a(tp, p, up)
        push_a(tp, p, down)
    push_b(ctx, 0, east)
    push_b(ctx, 1, west)
    for p in range(2):
        push_a(tp, p, line_dev[1])
    push_b(ctx, 1, east)
    push_b(ctx, 0, west)
    push_b(ctx, 0, sibling)
    push_b(ctx, 1, sibling)

    acc[...] = jnp.zeros_like(acc)
    sq[...] = jnp.zeros_like(sq)
    tap = lax.broadcasted_iota(jnp.int32, (TAPS, 2 * TAPS), 0)
    place = lax.broadcasted_iota(jnp.int32, (TAPS, 2 * TAPS), 1)
    flip = jnp.where(tap + place == TAPS, 1.0, 0.0).astype(BF16)
    flipped = jnp.dot(filt_ref[...], flip, preferred_element_type=F32)
    for g in range(GROUP):
        row = jnp.broadcast_to(flipped[g : g + 1, :], (TAPS, 2 * TAPS))
        toep[g * TAPS : (g + 1) * TAPS, :] = pltpu.roll(
            row, 0, 1, stride=1, stride_axis=0
        ).astype(BF16)
    absorb(tp)

    events = []

    def to_line(r):
        def act():
            for p in range(2):
                push_a(tp, p, line_dev[r])
        return act

    for r in (2, 3):
        events.append((LINE_GO_US[r], to_line(r)))

    for h in range(2):
        events.append((CROSS_GO_US[h], functools.partial(push_b, ctx, h, across)))

    halves = set()

    def from_z(r, p, d, sign, last):
        def act():
            t = lines[r] * 8 + lax.rem(z - sign * d + 8, 8)
            landed(*part(t, p))
            if d < last:
                push_a(t, p, up if sign > 0 else down)
            piece = (r, (-sign * d) % 8)
            if piece in halves:
                absorb(t)
            halves.add(piece)
        return act

    for sign in (1, -1):
        for at_us, r, p, d, last in ring_times(sign):
            events.append((at_us, from_z(r, p, d, sign, last)))

    def from_line(r):
        def act():
            t = lines[r] * 8 + z
            for p in range(2):
                landed(*part(t, p))
                push_a(t, p, up)
                push_a(t, p, down)
            absorb(t)
        return act

    for r in (1, 2, 3):
        events.append((LINE_US[r], from_line(r)))

    half_us = 8.4

    def from_x(dx, other, h, onward):
        def act():
            bx = lax.rem(x + dx + 4, 4)
            bh = (1 - yh) if other else yh
            block = (bx * 2 + bh) * 2 + core
            landed(*half(block, h))
            for device in onward:
                push_b(block, h, device)
            push_b(block, h, sibling)
        return act

    for other in (False, True):
        base0, base1 = CROSS_US if other else (0.0, 0.0)
        if other:
            events.append((base0, from_x(0, other, 0, (east, west))))
            events.append((base1, from_x(0, other, 1, (west, east))))
        events.append((base0 + half_us + 0.1, from_x(-1, other, 0, (east,))))
        events.append((base1 + half_us + 0.2, from_x(1, other, 1, (west,))))
        late0, late1 = (1, 1) if other else (2, 2)
        events.append((base1 + late1 * half_us + 0.3, from_x(-1, other, 1, ())))
        events.append((base0 + late0 * half_us + 0.4, from_x(1, other, 0, ())))
        far0, far1 = (2, 2) if other else (3, 3)
        events.append((base0 + far0 * half_us + 0.5, from_x(2, other, 0, ())))
        events.append((base1 + far1 * half_us + 0.5, from_x(2, other, 1, ())))

    def near_products(r, other_core):
        def act():
            block = (lines[r] * 2 + yh) * 2 + (1 - core if other_core else core)
            if other_core:
                for h in range(2):
                    landed(*half(block, h))
            multiply(block)
        return act

    for r in range(NEAR):
        for k, other_core in enumerate((False, True)):
            ready = max(t for sign in (1, -1) for t, q, *_ in ring_times(sign) if q == r)
            events.append((max(ready + 0.1, 33.0) + 2 * k, near_products(r, other_core)))

    def all_b(r):
        def act():
            for bh in (yh, 1 - yh) if r >= NEAR else (1 - yh,):
                block = (lines[r] * 2 + bh) * 2 + 1 - core
                for h in range(2):
                    landed(*half(block, h))
        return act

    def far_products(r, cc):
        def act():
            multiply((lines[r] * 2 + 1 - yh) * 2 + cc)
        return act

    def products(r, j):
        def act():
            multiply(lines[r] * 4 + lax.rem(lax.div(z, 2) + j, 4))
        return act

    three_hops = max(t for sign in (1, -1) for t, r, p, d, last in ring_times(sign) if d < 4)
    for r in range(4):
        events.append((ALL_B_US, all_b(r)))
    for r in range(NEAR):
        for cc in range(2):
            events.append((ALL_B_US + 0.9 * (2 * r + cc + 1), far_products(r, cc)))
    for r in range(NEAR, 4):
        events.append((ALL_B_US + 6, products(r, 0)))
        for j in (1, 3):
            assert ALL_B_US + 0.9 * 2 * NEAR < three_hops
            events.append((max(ALL_B_US + 6, three_hops + 0.1) + 0.01 * j, products(r, j)))
        events.append((200.0, products(r, 2)))
    for _, act in sorted(events, key=lambda event: event[0]):
        act()

    @pl.loop(0, ROWS // 128)
    def _(i):
        rows = pl.ds(pl.multiple_of(i * 128, 128), 128)
        total = jnp.sum(sq[rows, :], axis=1, keepdims=True)
        scale = lax.rsqrt(total / (PIECES * COLS) + 1e-06)
        for s in range(3):
            proj[pl.ds(pl.multiple_of(16 + i * 128, 16), 128), s * COLS : (s + 1) * COLS] = (
                acc[rows, s * COLS : (s + 1) * COLS] * scale
            ).astype(BF16)

    def feat(b, s):
        lines_ = pl.ds(pl.multiple_of(b * 128, 16), 144)
        block = proj[lines_, s * COLS : (s + 1) * COLS].astype(F32)
        return (
            sw_ref[0, s : s + 1, :] * block[16:144]
            + sw_ref[1, s : s + 1, :] * block[15:143]
            + sw_ref[2, s : s + 1, :] * block[14:142]
        )

    def gate(b):
        gated[pl.ds(pl.multiple_of((b + 1) * 128, 128), 128), :] = (feat(b, 1) * feat(b, 2)).astype(BF16)

    def mix(b):
        window = gated[pl.ds(pl.multiple_of(b * 128, 128), 256), :]
        lane = lax.broadcasted_iota(jnp.int32, (TAPS, COLS), 1)
        conv = jnp.zeros((TAPS, COLS), F32)
        for g in range(GROUP):
            part = jnp.dot(
                toep[g * TAPS : (g + 1) * TAPS, :], window, preferred_element_type=F32
            )
            inside = (lane >= g * GROUP) & (lane < (g + 1) * GROUP)
            conv = jnp.where(inside, part, conv)
        conv = conv.astype(BF16).astype(F32)
        out_ref[pl.ds(pl.multiple_of(b * 128, 128), 128), :] = (feat(b, 0) * conv).astype(BF16)

    gate(3)
    halo_out[0:TAPS, :] = gated[512:640, :]
    for s in range(3):
        halo_out[TAPS + 16 * s : TAPS + 16 * (s + 1), :] = proj[512:528, s * COLS : (s + 1) * COLS]
    push(halo_out, halo_in, halo_sem.at[0], after)

    gate(1)
    gate(2)
    mix(2)
    mix(3)
    landed(halo_in, halo_sem.at[0])
    keep = jnp.where(ctx > 0, 1.0, 0.0).astype(BF16)
    gated[0:TAPS, :] = halo_in[0:TAPS, :] * keep
    for s in range(3):
        proj[0:16, s * COLS : (s + 1) * COLS] = halo_in[TAPS + 16 * s : TAPS + 16 * (s + 1), :] * keep
    gate(0)
    mix(0)
    mix(1)
    for copy in sends:
        copy.wait_send()


N_SENDS = 120
MUL_ROWS = 256
NEAR = 3
LINE_GO_US = (0.0, 0.0, 0.1, 0.2)
LINE_US = (0.0, 12.0, 36.0, 58.0)
CROSS_GO_US = (24.0, 24.1)
CROSS_US = (54.0, 59.0)
ALL_B_US = 81.0


def ring_times(sign):
    part_us, delay_us = 3.2, 1.0
    waiting = []
    for r in range(4):
        for p in range(2):
            waiting.append((max(LINE_US[r], 0.0), r, p, 1))
    free, times = 0.0, []
    while waiting:
        waiting.sort()
        ready, r, p, d = waiting.pop(0)
        free = max(free, ready) + part_us
        last = 4 if (p == 0) == (sign > 0) else 3
        times.append((free + delay_us + (0.01 if sign < 0 else 0.0), r, p, d, last))
        if d < last:
            waiting.append((free + delay_us, r, p, d + 1))
    return times


def per_device(tokens, norm_gain, in_weight, short_weight, filters):
    weight = jnp.transpose(in_weight, (1, 0, 2))
    vmem = pl.BlockSpec(memory_space=pltpu.VMEM)
    hbm = pl.BlockSpec(memory_space=pl.ANY)
    return pl.pallas_call(
        kernel,
        out_shape=jax.ShapeDtypeStruct((ROWS, COLS), BF16),
        in_specs=[hbm, vmem, hbm, vmem, vmem],
        out_specs=vmem,
        scratch_shapes=[
            pltpu.VMEM((PIECES, EXT, COLS), BF16),
            pltpu.VMEM((PIECES // 2, 2 * COLS, 3 * COLS), BF16),
            pltpu.VMEM((PIECES // 2, ROWS, 2 * COLS), BF16),
            pltpu.VMEM((ROWS, 3 * COLS), F32),
            pltpu.VMEM((ROWS, 128), F32),
            pltpu.VMEM((GROUP * TAPS, 2 * TAPS), BF16),
            pltpu.VMEM((ROWS + 16, 3 * COLS), BF16),
            pltpu.VMEM((ROWS + TAPS, COLS), BF16),
            pltpu.VMEM((HALO, COLS), BF16),
            pltpu.VMEM((HALO, COLS), BF16),
            pltpu.SemaphoreType.DMA((4,)),
            pltpu.SemaphoreType.DMA((N_SENDS,)),
            pltpu.SemaphoreType.DMA((2 * PIECES,)),
            pltpu.SemaphoreType.DMA((PIECES,)),
            pltpu.SemaphoreType.DMA((1,)),
        ],
        compiler_params=pltpu.CompilerParams(
            collective_id=0, has_side_effects=True, vmem_limit_bytes=58 * 1024 * 1024
        ),
        cost_estimate=pl.CostEstimate(
            flops=2 * ROWS * 8192 * 768, bytes_accessed=4 * 1024 * 1024, transcendentals=0
        ),
    )(tokens, norm_gain, weight, short_weight, filters)


def solution(mesh):
    placed = (P("ctx", "tp"), P("tp"), P("ctx", None, "tp"), P(None, None, "tp"), P("tp", None))
    return jax.shard_map(
        per_device, mesh=mesh, in_specs=placed, out_specs=P("ctx", "tp"), check_vma=False
    )
```

```python
import functools

import jax
import jax.numpy as jnp
from jax import lax
from jax.experimental import pallas as pl
from jax.experimental.pallas import tpu as pltpu
from jax.sharding import PartitionSpec as P

MESH = pl.DeviceIdType.MESH
F32 = jnp.float32
BF16 = jnp.bfloat16
ROWS = 512
COLS = 256
PIECES = 32
TAPS = 128
GROUP = 16
EXT = ROWS + 16
HALO = TAPS + 48


def kernel(
    tok_ref, gain_ref, w_ref, sw_ref, filt_ref, out_ref,
    a_buf, b_buf, xg, acc, sq, toep, proj, gated, halo_out, halo_in,
    local_sem, send_sem, a_sem, b_sem, halo_sem,
):
    ctx = lax.axis_index("ctx")
    tp = lax.axis_index("tp")
    core = lax.rem(ctx, 2)
    yh = lax.rem(lax.div(ctx, 2), 2)
    x = lax.div(ctx, 4)
    z = lax.rem(tp, 8)
    yl = lax.div(tp, 8)
    y = yh * 4 + yl

    def at(dx=0, dy=0, dz=0):
        nx, ny, nz = lax.rem(x + dx + 4, 4), lax.rem(y + dy + 8, 8), lax.rem(z + dz + 8, 8)
        return ((nx * 2 + lax.div(ny, 4)) * 2 + core, lax.rem(ny, 4) * 8 + nz)

    lines = [yl, yl + 1 - 2 * lax.rem(yl, 2), lax.rem(yl + 2, 4), 3 - yl]
    line_dev = [(ctx, v * 8 + z) for v in lines]
    up, down = at(dz=1), at(dz=-1)
    east, west = at(dx=1), at(dx=-1)
    sibling = (ctx + 1 - 2 * core, tp)
    after, before = (lax.rem(ctx + 1, 16), tp), (lax.rem(ctx + 15, 16), tp)
    across = at(dy=4)

    sends = []

    def push(src, dst, sem, device):
        copy = pltpu.make_async_remote_copy(
            src_ref=src, dst_ref=dst, send_sem=send_sem.at[len(sends)], recv_sem=sem,
            device_id=device, device_id_type=MESH,
        )
        copy.start()
        sends.append(copy)

    def landed(slot, sem):
        pltpu.make_async_remote_copy(
            src_ref=slot, dst_ref=slot, send_sem=send_sem.at[0], recv_sem=sem,
            device_id=sibling, device_id_type=MESH,
        ).wait_recv()

    own = [
        pltpu.make_async_copy(tok_ref, a_buf.at[tp, pl.ds(0, ROWS)], local_sem.at[0]),
    ]
    for s in range(3):
        columns = pl.ds(s * COLS, COLS)
        own.append(
            pltpu.make_async_copy(w_ref.at[s], b_buf.at[ctx, :, columns], local_sem.at[1 + s])
        )
    for copy in own:
        copy.start()
    a_buf[tp, pl.ds(ROWS, 16), :] = jnp.broadcast_to(gain_ref[...].reshape(1, COLS), (16, COLS))

    barrier = pltpu.get_barrier_semaphore()
    peers = [up, down, east, west, sibling, after, before, across] + line_dev[1:]
    for peer in peers:
        pl.semaphore_signal(barrier, inc=1, device_id=peer, device_id_type=MESH)
    for copy in own:
        copy.wait()
    pl.semaphore_wait(barrier, len(peers))

    def part(t, p):
        rows = pl.ds(0, ROWS // 2) if p == 0 else pl.ds(ROWS // 2, ROWS // 2 + 16)
        return a_buf.at[t, rows], a_sem.at[2 * t + p]

    def push_a(t, p, device):
        ref, sem = part(t, p)
        push(ref, ref, sem, device)

    def half(block, h):
        return b_buf.at[block, pl.ds(h * 256, 256)], b_sem.at[2 * block + h]

    def push_b(block, h, device):
        ref, sem = half(block, h)
        push(ref, ref, sem, device)

    def absorb(t):
        gain = a_buf[t, pl.ds(ROWS, 16), :][0:1].astype(F32)
        columns = pl.ds(pl.multiple_of(lax.rem(t, 2) * COLS, COLS), COLS)

        @pl.loop(0, ROWS // 64)
        def _(i):
            rows = pl.ds(pl.multiple_of(i * 64, 64), 64)
            values = a_buf[t, rows, :].astype(F32)
            square = values * values
            sq[rows, :] += square[:, :128] + square[:, 128:]
            xg[lax.div(t, 2), rows, columns] = (values * gain).astype(BF16)

    def multiply(block):
        @pl.loop(0, ROWS // MUL_ROWS)
        def _(i):
            rows = pl.ds(pl.multiple_of(i * MUL_ROWS, MUL_ROWS), MUL_ROWS)
            acc[rows, :] += jnp.dot(xg[block, rows, :], b_buf[block], preferred_element_type=F32)

    for p in range(2):
        push_a(tp, p, up)
        push_a(tp, p, down)
    push_b(ctx, 0, east)
    push_b(ctx, 1, west)
    for p in range(2):
        push_a(tp, p, line_dev[1])
    push_b(ctx, 1, east)
    push_b(ctx, 0, west)
    push_b(ctx, 0, sibling)
    push_b(ctx, 1, sibling)

    acc[...] = jnp.zeros_like(acc)
    sq[...] = jnp.zeros_like(sq)
    tap = lax.broadcasted_iota(jnp.int32, (TAPS, 2 * TAPS), 0)
    place = lax.broadcasted_iota(jnp.int32, (TAPS, 2 * TAPS), 1)
    flip = jnp.where(tap + place == TAPS, 1.0, 0.0).astype(BF16)
    flipped = jnp.dot(filt_ref[...], flip, preferred_element_type=F32)
    for g in range(GROUP):
        row = jnp.broadcast_to(flipped[g : g + 1, :], (TAPS, 2 * TAPS))
        toep[g * TAPS : (g + 1) * TAPS, :] = pltpu.roll(
            row, 0, 1, stride=1, stride_axis=0
        ).astype(BF16)
    absorb(tp)

    events = []

    def to_line(r):
        def act():
            for p in range(2):
                push_a(tp, p, line_dev[r])
        return act

    for r in (2, 3):
        events.append((LINE_GO_US[r], to_line(r)))

    for h in range(2):
        events.append((CROSS_GO_US[h], functools.partial(push_b, ctx, h, across)))

    halves = set()

    def from_z(r, p, d, sign, last):
        def act():
            t = lines[r] * 8 + lax.rem(z - sign * d + 8, 8)
            landed(*part(t, p))
            if d < last:
                push_a(t, p, up if sign > 0 else down)
            piece = (r, (-sign * d) % 8)
            if piece in halves:
                absorb(t)
            halves.add(piece)
        return act

    for sign in (1, -1):
        for at_us, r, p, d, last in ring_times(sign):
            events.append((at_us, from_z(r, p, d, sign, last)))

    def from_line(r):
        def act():
            t = lines[r] * 8 + z
            for p in range(2):
                landed(*part(t, p))
                push_a(t, p, up)
                push_a(t, p, down)
            absorb(t)
        return act

    for r in (1, 2, 3):
        events.append((LINE_US[r], from_line(r)))

    half_us = 8.4

    def from_x(dx, other, h, onward):
        def act():
            bx = lax.rem(x + dx + 4, 4)
            bh = (1 - yh) if other else yh
            block = (bx * 2 + bh) * 2 + core
            landed(*half(block, h))
            for device in onward:
                push_b(block, h, device)
            push_b(block, h, sibling)
        return act

    for other in (False, True):
        base0, base1 = CROSS_US if other else (0.0, 0.0)
        if other:
            events.append((base0, from_x(0, other, 0, (east, west))))
            events.append((base1, from_x(0, other, 1, (west, east))))
        events.append((base0 + half_us + 0.1, from_x(-1, other, 0, (east,))))
        events.append((base1 + half_us + 0.2, from_x(1, other, 1, (west,))))
        late0, late1 = (1, 1) if other else (2, 2)
        events.append((base1 + late1 * half_us + 0.3, from_x(-1, other, 1, ())))
        events.append((base0 + late0 * half_us + 0.4, from_x(1, other, 0, ())))
        far0, far1 = (2, 2) if other else (3, 3)
        events.append((base0 + far0 * half_us + 0.5, from_x(2, other, 0, ())))
        events.append((base1 + far1 * half_us + 0.5, from_x(2, other, 1, ())))

    def near_products(r, other_core):
        def act():
            block = (lines[r] * 2 + yh) * 2 + (1 - core if other_core else core)
            if other_core:
                for h in range(2):
                    landed(*half(block, h))
            multiply(block)
        return act

    for r in range(NEAR):
        for k, other_core in enumerate((False, True)):
            ready = max(t for sign in (1, -1) for t, q, *_ in ring_times(sign) if q == r)
            events.append((max(ready + 0.1, 33.0) + 2 * k, near_products(r, other_core)))

    def all_b(r):
        def act():
            for bh in (yh, 1 - yh) if r >= NEAR else (1 - yh,):
                block = (lines[r] * 2 + bh) * 2 + 1 - core
                for h in range(2):
                    landed(*half(block, h))
        return act

    def far_products(r, cc):
        def act():
            multiply((lines[r] * 2 + 1 - yh) * 2 + cc)
        return act

    def products(r, j):
        def act():
            multiply(lines[r] * 4 + lax.rem(lax.div(z, 2) + j, 4))
        return act

    three_hops = max(t for sign in (1, -1) for t, r, p, d, last in ring_times(sign) if d < 4)
    for r in range(4):
        events.append((ALL_B_US, all_b(r)))
    for r in range(NEAR):
        for cc in range(2):
            events.append((ALL_B_US + 0.4 * (2 * r + cc + 1), far_products(r, cc)))
    for r in range(NEAR, 4):
        events.append((ALL_B_US + 2.6, products(r, 0)))
        for j in (1, 3):
            events.append((max(ALL_B_US + 2.7, three_hops + 0.1) + 0.01 * j, products(r, j)))
        events.append((200.0, products(r, 2)))
    for _, act in sorted(events, key=lambda event: event[0]):
        act()

    @pl.loop(0, ROWS // 128)
    def _(i):
        rows = pl.ds(pl.multiple_of(i * 128, 128), 128)
        total = jnp.sum(sq[rows, :], axis=1, keepdims=True)
        scale = lax.rsqrt(total / (PIECES * COLS) + 1e-06)
        for s in range(3):
            proj[pl.ds(pl.multiple_of(16 + i * 128, 16), 128), s * COLS : (s + 1) * COLS] = (
                acc[rows, s * COLS : (s + 1) * COLS] * scale
            ).astype(BF16)

    def feat(b, s):
        lines_ = pl.ds(pl.multiple_of(b * 128, 16), 144)
        block = proj[lines_, s * COLS : (s + 1) * COLS].astype(F32)
        return (
            sw_ref[0, s : s + 1, :] * block[16:144]
            + sw_ref[1, s : s + 1, :] * block[15:143]
            + sw_ref[2, s : s + 1, :] * block[14:142]
        )

    def gate(b):
        gated[pl.ds(pl.multiple_of((b + 1) * 128, 128), 128), :] = (feat(b, 1) * feat(b, 2)).astype(BF16)

    def mix(b):
        window = gated[pl.ds(pl.multiple_of(b * 128, 128), 256), :]
        lane = lax.broadcasted_iota(jnp.int32, (TAPS, COLS), 1)
        conv = jnp.zeros((TAPS, COLS), F32)
        for g in range(GROUP):
            part = jnp.dot(
                toep[g * TAPS : (g + 1) * TAPS, :], window, preferred_element_type=F32
            )
            inside = (lane >= g * GROUP) & (lane < (g + 1) * GROUP)
            conv = jnp.where(inside, part, conv)
        conv = conv.astype(BF16).astype(F32)
        out_ref[pl.ds(pl.multiple_of(b * 128, 128), 128), :] = (feat(b, 0) * conv).astype(BF16)

    gate(3)
    halo_out[0:TAPS, :] = gated[512:640, :]
    for s in range(3):
        halo_out[TAPS + 16 * s : TAPS + 16 * (s + 1), :] = proj[512:528, s * COLS : (s + 1) * COLS]
    push(halo_out, halo_in, halo_sem.at[0], after)

    gate(1)
    gate(2)
    mix(2)
    mix(3)
    landed(halo_in, halo_sem.at[0])
    keep = jnp.where(ctx > 0, 1.0, 0.0).astype(BF16)
    gated[0:TAPS, :] = halo_in[0:TAPS, :] * keep
    for s in range(3):
        proj[0:16, s * COLS : (s + 1) * COLS] = halo_in[TAPS + 16 * s : TAPS + 16 * (s + 1), :] * keep
    gate(0)
    mix(0)
    mix(1)
    for copy in sends:
        copy.wait_send()


N_SENDS = 120
MUL_ROWS = 256
NEAR = 3
LINE_GO_US = (0.0, 0.0, 0.1, 0.2)
LINE_US = (0.0, 12.0, 36.0, 58.0)
CROSS_GO_US = (24.0, 24.1)
CROSS_US = (50.0, 52.0)
ALL_B_US = 84.6


def ring_times(sign):
    part_us, delay_us = 3.2, 1.0
    waiting = []
    for r in range(4):
        for p in range(2):
            waiting.append((max(LINE_US[r], 0.0), r, p, 1))
    free, times = 0.0, []
    while waiting:
        waiting.sort()
        ready, r, p, d = waiting.pop(0)
        free = max(free, ready) + part_us
        last = 4 if (p == 0) == (sign > 0) else 3
        times.append((free + delay_us + (0.01 if sign < 0 else 0.0), r, p, d, last))
        if d < last:
            waiting.append((free + delay_us, r, p, d + 1))
    return times


def per_device(tokens, norm_gain, in_weight, short_weight, filters):
    weight = jnp.transpose(in_weight, (1, 0, 2))
    vmem = pl.BlockSpec(memory_space=pltpu.VMEM)
    hbm = pl.BlockSpec(memory_space=pl.ANY)
    return pl.pallas_call(
        kernel,
        out_shape=jax.ShapeDtypeStruct((ROWS, COLS), BF16),
        in_specs=[hbm, vmem, hbm, vmem, vmem],
        out_specs=vmem,
        scratch_shapes=[
            pltpu.VMEM((PIECES, EXT, COLS), BF16),
            pltpu.VMEM((PIECES // 2, 2 * COLS, 3 * COLS), BF16),
            pltpu.VMEM((PIECES // 2, ROWS, 2 * COLS), BF16),
            pltpu.VMEM((ROWS, 3 * COLS), F32),
            pltpu.VMEM((ROWS, 128), F32),
            pltpu.VMEM((GROUP * TAPS, 2 * TAPS), BF16),
            pltpu.VMEM((ROWS + 16, 3 * COLS), BF16),
            pltpu.VMEM((ROWS + TAPS, COLS), BF16),
            pltpu.VMEM((HALO, COLS), BF16),
            pltpu.VMEM((HALO, COLS), BF16),
            pltpu.SemaphoreType.DMA((4,)),
            pltpu.SemaphoreType.DMA((N_SENDS,)),
            pltpu.SemaphoreType.DMA((2 * PIECES,)),
            pltpu.SemaphoreType.DMA((PIECES,)),
            pltpu.SemaphoreType.DMA((1,)),
        ],
        compiler_params=pltpu.CompilerParams(
            collective_id=0, has_side_effects=True, vmem_limit_bytes=58 * 1024 * 1024
        ),
        cost_estimate=pl.CostEstimate(
            flops=2 * ROWS * 8192 * 768, bytes_accessed=4 * 1024 * 1024, transcendentals=0
        ),
    )(tokens, norm_gain, weight, short_weight, filters)


def solution(mesh):
    placed = (P("ctx", "tp"), P("tp"), P("ctx", None, "tp"), P(None, None, "tp"), P("tp", None))
    return jax.shard_map(
        per_device, mesh=mesh, in_specs=placed, out_specs=P("ctx", "tp"), check_vma=False
    )
```

```python
import functools

import jax
import jax.numpy as jnp
from jax import lax
from jax.experimental import pallas as pl
from jax.experimental.pallas import tpu as pltpu
from jax.sharding import PartitionSpec as P

MESH = pl.DeviceIdType.MESH
F32 = jnp.float32
BF16 = jnp.bfloat16
ROWS = 512
COLS = 256
PIECES = 32
TAPS = 128
GROUP = 16
EXT = ROWS + 16
HALO = TAPS + 48


def kernel(
    tok_ref, gain_ref, w_ref, sw_ref, filt_ref, out_ref,
    a_buf, b_buf, xg, acc, sq, toep, proj, gated, halo_out, halo_in,
    local_sem, send_sem, a_sem, b_sem, halo_sem,
):
    ctx = lax.axis_index("ctx")
    tp = lax.axis_index("tp")
    core = lax.rem(ctx, 2)
    yh = lax.rem(lax.div(ctx, 2), 2)
    x = lax.div(ctx, 4)
    z = lax.rem(tp, 8)
    yl = lax.div(tp, 8)
    y = yh * 4 + yl

    def at(dx=0, dy=0, dz=0):
        nx, ny, nz = lax.rem(x + dx + 4, 4), lax.rem(y + dy + 8, 8), lax.rem(z + dz + 8, 8)
        return ((nx * 2 + lax.div(ny, 4)) * 2 + core, lax.rem(ny, 4) * 8 + nz)

    lines = [yl, yl + 1 - 2 * lax.rem(yl, 2), lax.rem(yl + 2, 4), 3 - yl]
    line_dev = [(ctx, v * 8 + z) for v in lines]
    up, down = at(dz=1), at(dz=-1)
    east, west = at(dx=1), at(dx=-1)
    sibling = (ctx + 1 - 2 * core, tp)
    after, before = (lax.rem(ctx + 1, 16), tp), (lax.rem(ctx + 15, 16), tp)
    across = at(dy=4)

    sends = []

    def push(src, dst, sem, device):
        copy = pltpu.make_async_remote_copy(
            src_ref=src, dst_ref=dst, send_sem=send_sem.at[len(sends)], recv_sem=sem,
            device_id=device, device_id_type=MESH,
        )
        copy.start()
        sends.append(copy)

    def landed(slot, sem):
        pltpu.make_async_remote_copy(
            src_ref=slot, dst_ref=slot, send_sem=send_sem.at[0], recv_sem=sem,
            device_id=sibling, device_id_type=MESH,
        ).wait_recv()

    own = [
        pltpu.make_async_copy(tok_ref, a_buf.at[tp, pl.ds(0, ROWS)], local_sem.at[0]),
    ]
    for s in range(3):
        columns = pl.ds(s * COLS, COLS)
        own.append(
            pltpu.make_async_copy(w_ref.at[s], b_buf.at[ctx, :, columns], local_sem.at[1 + s])
        )
    for copy in own:
        copy.start()
    a_buf[tp, pl.ds(ROWS, 16), :] = jnp.broadcast_to(gain_ref[...].reshape(1, COLS), (16, COLS))

    barrier = pltpu.get_barrier_semaphore()
    peers = [up, down, east, west, sibling, after, before, across] + line_dev[1:]
    for peer in peers:
        pl.semaphore_signal(barrier, inc=1, device_id=peer, device_id_type=MESH)
    for copy in own:
        copy.wait()
    pl.semaphore_wait(barrier, len(peers))

    def part(t, p):
        rows = pl.ds(0, ROWS // 2) if p == 0 else pl.ds(ROWS // 2, ROWS // 2 + 16)
        return a_buf.at[t, rows], a_sem.at[2 * t + p]

    def push_a(t, p, device):
        ref, sem = part(t, p)
        push(ref, ref, sem, device)

    def half(block, h):
        return b_buf.at[block, pl.ds(h * 256, 256)], b_sem.at[2 * block + h]

    def push_b(block, h, device):
        ref, sem = half(block, h)
        push(ref, ref, sem, device)

    def absorb(t):
        gain = a_buf[t, pl.ds(ROWS, 16), :][0:1].astype(F32)
        columns = pl.ds(pl.multiple_of(lax.rem(t, 2) * COLS, COLS), COLS)

        @pl.loop(0, ROWS // 64)
        def _(i):
            rows = pl.ds(pl.multiple_of(i * 64, 64), 64)
            values = a_buf[t, rows, :].astype(F32)
            square = values * values
            sq[rows, :] += square[:, :128] + square[:, 128:]
            xg[lax.div(t, 2), rows, columns] = (values * gain).astype(BF16)

    def multiply(block):
        @pl.loop(0, ROWS // MUL_ROWS)
        def _(i):
            rows = pl.ds(pl.multiple_of(i * MUL_ROWS, MUL_ROWS), MUL_ROWS)
            acc[rows, :] += jnp.dot(xg[block, rows, :], b_buf[block], preferred_element_type=F32)

    for p in range(2):
        push_a(tp, p, up)
        push_a(tp, p, down)
    push_b(ctx, 0, east)
    push_b(ctx, 1, west)
    for p in range(2):
        push_a(tp, p, line_dev[1])
    push_b(ctx, 1, east)
    push_b(ctx, 0, west)
    push_b(ctx, 0, sibling)
    push_b(ctx, 1, sibling)

    acc[...] = jnp.zeros_like(acc)
    sq[...] = jnp.zeros_like(sq)
    tap = lax.broadcasted_iota(jnp.int32, (TAPS, 2 * TAPS), 0)
    place = lax.broadcasted_iota(jnp.int32, (TAPS, 2 * TAPS), 1)
    flip = jnp.where(tap + place == TAPS, 1.0, 0.0).astype(BF16)
    flipped = jnp.dot(filt_ref[...], flip, preferred_element_type=F32)
    for g in range(GROUP):
        row = jnp.broadcast_to(flipped[g : g + 1, :], (TAPS, 2 * TAPS))
        toep[g * TAPS : (g + 1) * TAPS, :] = pltpu.roll(
            row, 0, 1, stride=1, stride_axis=0
        ).astype(BF16)
    absorb(tp)

    events = []

    def to_line(r):
        def act():
            for p in range(2):
                push_a(tp, p, line_dev[r])
        return act

    for r in (2, 3):
        events.append((LINE_GO_US[r], to_line(r)))

    for h in range(2):
        events.append((CROSS_GO_US[h], functools.partial(push_b, ctx, h, across)))

    halves = set()

    def from_z(r, p, d, sign, last):
        def act():
            t = lines[r] * 8 + lax.rem(z - sign * d + 8, 8)
            landed(*part(t, p))
            if d < last:
                push_a(t, p, up if sign > 0 else down)
            piece = (r, (-sign * d) % 8)
            if piece in halves:
                absorb(t)
            halves.add(piece)
        return act

    for sign in (1, -1):
        for at_us, r, p, d, last in ring_times(sign):
            events.append((at_us, from_z(r, p, d, sign, last)))

    def from_line(r):
        def act():
            t = lines[r] * 8 + z
            for p in range(2):
                landed(*part(t, p))
                push_a(t, p, up)
                push_a(t, p, down)
            absorb(t)
        return act

    for r in (1, 2, 3):
        events.append((LINE_US[r], from_line(r)))

    half_us = 8.4

    def from_x(dx, other, h, onward):
        def act():
            bx = lax.rem(x + dx + 4, 4)
            bh = (1 - yh) if other else yh
            block = (bx * 2 + bh) * 2 + core
            landed(*half(block, h))
            for device in onward:
                push_b(block, h, device)
            push_b(block, h, sibling)
        return act

    for other in (False, True):
        base0, base1 = CROSS_US if other else (0.0, 0.0)
        if other:
            events.append((base0, from_x(0, other, 0, (east, west))))
            events.append((base1, from_x(0, other, 1, (west, east))))
        events.append((base0 + half_us + 0.1, from_x(-1, other, 0, (east,))))
        events.append((base1 + half_us + 0.2, from_x(1, other, 1, (west,))))
        late0, late1 = (1, 1) if other else (2, 2)
        events.append((base1 + late1 * half_us + 0.3, from_x(-1, other, 1, ())))
        events.append((base0 + late0 * half_us + 0.4, from_x(1, other, 0, ())))
        far0, far1 = (2, 2) if other else (3, 3)
        events.append((base0 + far0 * half_us + 0.5, from_x(2, other, 0, ())))
        events.append((base1 + far1 * half_us + 0.5, from_x(2, other, 1, ())))

    def near_products(r, other_core):
        def act():
            block = (lines[r] * 2 + yh) * 2 + (1 - core if other_core else core)
            if other_core:
                for h in range(2):
                    landed(*half(block, h))
            multiply(block)
        return act

    for r in range(NEAR):
        for k, other_core in enumerate((False, True)):
            ready = max(t for sign in (1, -1) for t, q, *_ in ring_times(sign) if q == r)
            events.append((max(ready + 0.1, 33.0) + 2 * k, near_products(r, other_core)))

    def all_b(r):
        def act():
            for bh in (yh, 1 - yh) if r >= NEAR else (1 - yh,):
                block = (lines[r] * 2 + bh) * 2 + 1 - core
                for h in range(2):
                    landed(*half(block, h))
        return act

    def far_products(r, cc):
        def act():
            multiply((lines[r] * 2 + 1 - yh) * 2 + cc)
        return act

    def products(r, j):
        def act():
            multiply(lines[r] * 4 + lax.rem(lax.div(z, 2) + j, 4))
        return act

    three_hops = max(t for sign in (1, -1) for t, r, p, d, last in ring_times(sign) if d < 4)
    for r in range(4):
        events.append((ALL_B_US, all_b(r)))
    for r in range(NEAR):
        for cc in range(2):
            events.append((ALL_B_US + 0.4 * (2 * r + cc + 1), far_products(r, cc)))
    for r in range(NEAR, 4):
        events.append((ALL_B_US + 2.6, products(r, 0)))
        for j in (1, 3):
            events.append((max(ALL_B_US + 2.7, three_hops + 0.1) + 0.01 * j, products(r, j)))
        events.append((200.0, products(r, 2)))
    for _, act in sorted(events, key=lambda event: event[0]):
        act()

    @pl.loop(0, ROWS // 128)
    def _(i):
        rows = pl.ds(pl.multiple_of(i * 128, 128), 128)
        total = jnp.sum(sq[rows, :], axis=1, keepdims=True)
        scale = lax.rsqrt(total / (PIECES * COLS) + 1e-06)
        for s in range(3):
            proj[pl.ds(pl.multiple_of(16 + i * 128, 16), 128), s * COLS : (s + 1) * COLS] = (
                acc[rows, s * COLS : (s + 1) * COLS] * scale
            ).astype(BF16)

    def feat(b, s):
        lines_ = pl.ds(pl.multiple_of(b * 128, 16), 144)
        block = proj[lines_, s * COLS : (s + 1) * COLS].astype(F32)
        return (
            sw_ref[0, s : s + 1, :] * block[16:144]
            + sw_ref[1, s : s + 1, :] * block[15:143]
            + sw_ref[2, s : s + 1, :] * block[14:142]
        )

    def gate(b):
        gated[pl.ds(pl.multiple_of((b + 1) * 128, 128), 128), :] = (feat(b, 1) * feat(b, 2)).astype(BF16)

    def mix(b):
        window = gated[pl.ds(pl.multiple_of(b * 128, 128), 256), :]
        lane = lax.broadcasted_iota(jnp.int32, (TAPS, COLS), 1)
        conv = jnp.zeros((TAPS, COLS), F32)
        for g in range(GROUP):
            part = jnp.dot(
                toep[g * TAPS : (g + 1) * TAPS, :], window, preferred_element_type=F32
            )
            inside = (lane >= g * GROUP) & (lane < (g + 1) * GROUP)
            conv = jnp.where(inside, part, conv)
        conv = conv.astype(BF16).astype(F32)
        out_ref[pl.ds(pl.multiple_of(b * 128, 128), 128), :] = (feat(b, 0) * conv).astype(BF16)

    gate(3)
    halo_out[0:TAPS, :] = gated[512:640, :]
    for s in range(3):
        halo_out[TAPS + 16 * s : TAPS + 16 * (s + 1), :] = proj[512:528, s * COLS : (s + 1) * COLS]
    push(halo_out, halo_in, halo_sem.at[0], after)

    gate(1)
    gate(2)
    mix(2)
    mix(3)
    landed(halo_in, halo_sem.at[0])
    keep = jnp.where(ctx > 0, 1.0, 0.0).astype(BF16)
    gated[0:TAPS, :] = halo_in[0:TAPS, :] * keep
    for s in range(3):
        proj[0:16, s * COLS : (s + 1) * COLS] = halo_in[TAPS + 16 * s : TAPS + 16 * (s + 1), :] * keep
    gate(0)
    mix(0)
    mix(1)
    for copy in sends:
        copy.wait_send()


N_SENDS = 120
MUL_ROWS = 256
NEAR = 3
LINE_GO_US = (0.0, 0.0, 0.1, 0.2)
LINE_US = (0.0, 12.0, 36.0, 58.0)
CROSS_GO_US = (24.0, 24.1)
CROSS_US = (56.0, 58.5)
ALL_B_US = 84.6


def ring_times(sign):
    part_us, delay_us = 3.2, 1.0
    waiting = []
    for r in range(4):
        for p in range(2):
            waiting.append((max(LINE_US[r], 0.0), r, p, 1))
    free, times = 0.0, []
    while waiting:
        waiting.sort()
        ready, r, p, d = waiting.pop(0)
        free = max(free, ready) + part_us
        last = 4 if (p == 0) == (sign > 0) else 3
        times.append((free + delay_us + (0.01 if sign < 0 else 0.0), r, p, d, last))
        if d < last:
            waiting.append((free + delay_us, r, p, d + 1))
    return times


def per_device(tokens, norm_gain, in_weight, short_weight, filters):
    weight = jnp.transpose(in_weight, (1, 0, 2))
    vmem = pl.BlockSpec(memory_space=pltpu.VMEM)
    hbm = pl.BlockSpec(memory_space=pl.ANY)
    return pl.pallas_call(
        kernel,
        out_shape=jax.ShapeDtypeStruct((ROWS, COLS), BF16),
        in_specs=[hbm, vmem, hbm, vmem, vmem],
        out_specs=vmem,
        scratch_shapes=[
            pltpu.VMEM((PIECES, EXT, COLS), BF16),
            pltpu.VMEM((PIECES // 2, 2 * COLS, 3 * COLS), BF16),
            pltpu.VMEM((PIECES // 2, ROWS, 2 * COLS), BF16),
            pltpu.VMEM((ROWS, 3 * COLS), F32),
            pltpu.VMEM((ROWS, 128), F32),
            pltpu.VMEM((GROUP * TAPS, 2 * TAPS), BF16),
            pltpu.VMEM((ROWS + 16, 3 * COLS), BF16),
            pltpu.VMEM((ROWS + TAPS, COLS), BF16),
            pltpu.VMEM((HALO, COLS), BF16),
            pltpu.VMEM((HALO, COLS), BF16),
            pltpu.SemaphoreType.DMA((4,)),
            pltpu.SemaphoreType.DMA((N_SENDS,)),
            pltpu.SemaphoreType.DMA((2 * PIECES,)),
            pltpu.SemaphoreType.DMA((PIECES,)),
            pltpu.SemaphoreType.DMA((1,)),
        ],
        compiler_params=pltpu.CompilerParams(
            collective_id=0, has_side_effects=True, vmem_limit_bytes=58 * 1024 * 1024
        ),
        cost_estimate=pl.CostEstimate(
            flops=2 * ROWS * 8192 * 768, bytes_accessed=4 * 1024 * 1024, transcendentals=0
        ),
    )(tokens, norm_gain, weight, short_weight, filters)


def solution(mesh):
    placed = (P("ctx", "tp"), P("tp"), P("ctx", None, "tp"), P(None, None, "tp"), P("tp", None))
    return jax.shard_map(
        per_device, mesh=mesh, in_specs=placed, out_specs=P("ctx", "tp"), check_vma=False
    )
```

```python
import functools

import jax
import jax.numpy as jnp
from jax import lax
from jax.experimental import pallas as pl
from jax.experimental.pallas import tpu as pltpu
from jax.sharding import PartitionSpec as P

MESH = pl.DeviceIdType.MESH
F32 = jnp.float32
BF16 = jnp.bfloat16
ROWS = 512
COLS = 256
PIECES = 32
TAPS = 128
GROUP = 16
EXT = ROWS + 16
HALO = TAPS + 48


def kernel(
    tok_ref, gain_ref, w_ref, sw_ref, filt_ref, out_ref,
    a_buf, b_buf, xg, acc, sq, toep, proj, gated, halo_out, halo_in,
    local_sem, send_sem, a_sem, b_sem, halo_sem,
):
    ctx = lax.axis_index("ctx")
    tp = lax.axis_index("tp")
    core = lax.rem(ctx, 2)
    yh = lax.rem(lax.div(ctx, 2), 2)
    x = lax.div(ctx, 4)
    z = lax.rem(tp, 8)
    yl = lax.div(tp, 8)
    y = yh * 4 + yl

    def at(dx=0, dy=0, dz=0):
        nx, ny, nz = lax.rem(x + dx + 4, 4), lax.rem(y + dy + 8, 8), lax.rem(z + dz + 8, 8)
        return ((nx * 2 + lax.div(ny, 4)) * 2 + core, lax.rem(ny, 4) * 8 + nz)

    lines = [yl, yl + 1 - 2 * lax.rem(yl, 2), lax.rem(yl + 2, 4), 3 - yl]
    line_dev = [(ctx, v * 8 + z) for v in lines]
    up, down = at(dz=1), at(dz=-1)
    east, west = at(dx=1), at(dx=-1)
    sibling = (ctx + 1 - 2 * core, tp)
    after, before = (lax.rem(ctx + 1, 16), tp), (lax.rem(ctx + 15, 16), tp)
    across = at(dy=4)

    sends = []

    def push(src, dst, sem, device):
        copy = pltpu.make_async_remote_copy(
            src_ref=src, dst_ref=dst, send_sem=send_sem.at[len(sends)], recv_sem=sem,
            device_id=device, device_id_type=MESH,
        )
        copy.start()
        sends.append(copy)

    def landed(slot, sem):
        pltpu.make_async_remote_copy(
            src_ref=slot, dst_ref=slot, send_sem=send_sem.at[0], recv_sem=sem,
            device_id=sibling, device_id_type=MESH,
        ).wait_recv()

    own = [
        pltpu.make_async_copy(tok_ref, a_buf.at[tp, pl.ds(0, ROWS)], local_sem.at[0]),
    ]
    for s in range(3):
        columns = pl.ds(s * COLS, COLS)
        own.append(
            pltpu.make_async_copy(w_ref.at[s], b_buf.at[ctx, :, columns], local_sem.at[1 + s])
        )
    for copy in own:
        copy.start()
    a_buf[tp, pl.ds(ROWS, 16), :] = jnp.broadcast_to(gain_ref[...].reshape(1, COLS), (16, COLS))

    barrier = pltpu.get_barrier_semaphore()
    peers = [up, down, east, west, sibling, after, before, across] + line_dev[1:]
    for peer in peers:
        pl.semaphore_signal(barrier, inc=1, device_id=peer, device_id_type=MESH)
    for copy in own:
        copy.wait()
    pl.semaphore_wait(barrier, len(peers))

    def part(t, p):
        rows = pl.ds(0, ROWS // 2) if p == 0 else pl.ds(ROWS // 2, ROWS // 2 + 16)
        return a_buf.at[t, rows], a_sem.at[2 * t + p]

    def push_a(t, p, device):
        ref, sem = part(t, p)
        push(ref, ref, sem, device)

    def half(block, h):
        return b_buf.at[block, pl.ds(h * 256, 256)], b_sem.at[2 * block + h]

    def push_b(block, h, device):
        ref, sem = half(block, h)
        push(ref, ref, sem, device)

    def absorb(t):
        gain = a_buf[t, pl.ds(ROWS, 16), :][0:1].astype(F32)
        columns = pl.ds(pl.multiple_of(lax.rem(t, 2) * COLS, COLS), COLS)

        @pl.loop(0, ROWS // 64)
        def _(i):
            rows = pl.ds(pl.multiple_of(i * 64, 64), 64)
            values = a_buf[t, rows, :].astype(F32)
            square = values * values
            sq[rows, :] += square[:, :128] + square[:, 128:]
            xg[lax.div(t, 2), rows, columns] = (values * gain).astype(BF16)

    def multiply(block):
        @pl.loop(0, ROWS // MUL_ROWS)
        def _(i):
            rows = pl.ds(pl.multiple_of(i * MUL_ROWS, MUL_ROWS), MUL_ROWS)
            acc[rows, :] += jnp.dot(xg[block, rows, :], b_buf[block], preferred_element_type=F32)

    for p in range(2):
        push_a(tp, p, up)
        push_a(tp, p, down)
    push_b(ctx, 0, east)
    push_b(ctx, 1, west)
    for p in range(2):
        push_a(tp, p, line_dev[1])
    push_b(ctx, 1, east)
    push_b(ctx, 0, west)
    push_b(ctx, 0, sibling)
    push_b(ctx, 1, sibling)

    acc[...] = jnp.zeros_like(acc)
    sq[...] = jnp.zeros_like(sq)
    tap = lax.broadcasted_iota(jnp.int32, (TAPS, 2 * TAPS), 0)
    place = lax.broadcasted_iota(jnp.int32, (TAPS, 2 * TAPS), 1)
    flip = jnp.where(tap + place == TAPS, 1.0, 0.0).astype(BF16)
    flipped = jnp.dot(filt_ref[...], flip, preferred_element_type=F32)
    for g in range(GROUP):
        row = jnp.broadcast_to(flipped[g : g + 1, :], (TAPS, 2 * TAPS))
        toep[g * TAPS : (g + 1) * TAPS, :] = pltpu.roll(
            row, 0, 1, stride=1, stride_axis=0
        ).astype(BF16)
    absorb(tp)

    events = []

    def to_line(r):
        def act():
            for p in range(2):
                push_a(tp, p, line_dev[r])
        return act

    for r in (2, 3):
        events.append((LINE_GO_US[r], to_line(r)))

    for h in range(2):
        events.append((CROSS_GO_US[h], functools.partial(push_b, ctx, h, across)))

    halves = set()

    def from_z(r, p, d, sign, last):
        def act():
            t = lines[r] * 8 + lax.rem(z - sign * d + 8, 8)
            landed(*part(t, p))
            if d < last:
                push_a(t, p, up if sign > 0 else down)
            piece = (r, (-sign * d) % 8)
            if piece in halves:
                absorb(t)
            halves.add(piece)
        return act

    for sign in (1, -1):
        for at_us, r, p, d, last in ring_times(sign):
            events.append((at_us, from_z(r, p, d, sign, last)))

    def from_line(r):
        def act():
            t = lines[r] * 8 + z
            for p in range(2):
                landed(*part(t, p))
                push_a(t, p, up)
                push_a(t, p, down)
            absorb(t)
        return act

    for r in (1, 2, 3):
        events.append((LINE_US[r], from_line(r)))

    half_us = 8.4

    def from_x(dx, other, h, onward):
        def act():
            bx = lax.rem(x + dx + 4, 4)
            bh = (1 - yh) if other else yh
            block = (bx * 2 + bh) * 2 + core
            landed(*half(block, h))
            for device in onward:
                push_b(block, h, device)
            push_b(block, h, sibling)
        return act

    for other in (False, True):
        base0, base1 = CROSS_US if other else (0.0, 0.0)
        if other:
            events.append((base0, from_x(0, other, 0, (east, west))))
            events.append((base1, from_x(0, other, 1, (west, east))))
        events.append((base0 + half_us + 0.1, from_x(-1, other, 0, (east,))))
        events.append((base1 + half_us + 0.2, from_x(1, other, 1, (west,))))
        late0, late1 = (1, 1) if other else (2, 2)
        events.append((base1 + late1 * half_us + 0.3, from_x(-1, other, 1, ())))
        events.append((base0 + late0 * half_us + 0.4, from_x(1, other, 0, ())))
        far0, far1 = (2, 2) if other else (3, 3)
        events.append((base0 + far0 * half_us + 0.5, from_x(2, other, 0, ())))
        events.append((base1 + far1 * half_us + 0.5, from_x(2, other, 1, ())))

    def near_products(r, other_core):
        def act():
            block = (lines[r] * 2 + yh) * 2 + (1 - core if other_core else core)
            if other_core:
                for h in range(2):
                    landed(*half(block, h))
            multiply(block)
        return act

    for r in range(NEAR):
        for k, other_core in enumerate((False, True)):
            ready = max(t for sign in (1, -1) for t, q, *_ in ring_times(sign) if q == r)
            events.append((max(ready + 0.1, 33.0) + 2 * k, near_products(r, other_core)))

    def all_b(r):
        def act():
            for bh in (yh, 1 - yh) if r >= NEAR else (1 - yh,):
                block = (lines[r] * 2 + bh) * 2 + 1 - core
                for h in range(2):
                    landed(*half(block, h))
        return act

    def far_products(r, cc):
        def act():
            multiply((lines[r] * 2 + 1 - yh) * 2 + cc)
        return act

    def products(r, j):
        def act():
            multiply(lines[r] * 4 + lax.rem(lax.div(z, 2) + j, 4))
        return act

    three_hops = max(t for sign in (1, -1) for t, r, p, d, last in ring_times(sign) if d < 4)
    for r in range(4):
        events.append((ALL_B_US, all_b(r)))
    for r in range(NEAR):
        for cc in range(2):
            events.append((ALL_B_US + 0.4 * (2 * r + cc + 1), far_products(r, cc)))
    for r in range(NEAR, 4):
        events.append((ALL_B_US + 2.6, products(r, 0)))
        for j in (1, 3):
            events.append((max(ALL_B_US + 2.7, three_hops + 0.1) + 0.01 * j, products(r, j)))
        events.append((200.0, products(r, 2)))
    for _, act in sorted(events, key=lambda event: event[0]):
        act()

    @pl.loop(0, ROWS // 128)
    def _(i):
        rows = pl.ds(pl.multiple_of(i * 128, 128), 128)
        total = jnp.sum(sq[rows, :], axis=1, keepdims=True)
        scale = lax.rsqrt(total / (PIECES * COLS) + 1e-06)
        for s in range(3):
            proj[pl.ds(pl.multiple_of(16 + i * 128, 16), 128), s * COLS : (s + 1) * COLS] = (
                acc[rows, s * COLS : (s + 1) * COLS] * scale
            ).astype(BF16)

    def feat(b, s):
        lines_ = pl.ds(pl.multiple_of(b * 128, 16), 144)
        block = proj[lines_, s * COLS : (s + 1) * COLS].astype(F32)
        return (
            sw_ref[0, s : s + 1, :] * block[16:144]
            + sw_ref[1, s : s + 1, :] * block[15:143]
            + sw_ref[2, s : s + 1, :] * block[14:142]
        )

    def gate(b):
        gated[pl.ds(pl.multiple_of((b + 1) * 128, 128), 128), :] = (feat(b, 1) * feat(b, 2)).astype(BF16)

    def mix(b):
        window = gated[pl.ds(pl.multiple_of(b * 128, 128), 256), :]
        lane = lax.broadcasted_iota(jnp.int32, (TAPS, COLS), 1)
        conv = jnp.zeros((TAPS, COLS), F32)
        for g in range(GROUP):
            part = jnp.dot(
                toep[g * TAPS : (g + 1) * TAPS, :], window, preferred_element_type=F32
            )
            inside = (lane >= g * GROUP) & (lane < (g + 1) * GROUP)
            conv = jnp.where(inside, part, conv)
        conv = conv.astype(BF16).astype(F32)
        out_ref[pl.ds(pl.multiple_of(b * 128, 128), 128), :] = (feat(b, 0) * conv).astype(BF16)

    gate(3)
    halo_out[0:TAPS, :] = gated[512:640, :]
    for s in range(3):
        halo_out[TAPS + 16 * s : TAPS + 16 * (s + 1), :] = proj[512:528, s * COLS : (s + 1) * COLS]
    push(halo_out, halo_in, halo_sem.at[0], after)

    gate(1)
    gate(2)
    mix(2)
    mix(3)
    landed(halo_in, halo_sem.at[0])
    keep = jnp.where(ctx > 0, 1.0, 0.0).astype(BF16)
    gated[0:TAPS, :] = halo_in[0:TAPS, :] * keep
    for s in range(3):
        proj[0:16, s * COLS : (s + 1) * COLS] = halo_in[TAPS + 16 * s : TAPS + 16 * (s + 1), :] * keep
    gate(0)
    mix(0)
    mix(1)
    for copy in sends:
        copy.wait_send()


N_SENDS = 120
MUL_ROWS = 256
NEAR = 3
LINE_GO_US = (0.0, 0.0, 0.1, 32.0)
LINE_US = (0.0, 12.0, 36.0, 58.0)
CROSS_GO_US = (15.0, 15.1)
CROSS_US = (50.0, 54.0)
ALL_B_US = 84.6


def ring_times(sign):
    part_us, delay_us = 3.2, 1.0
    waiting = []
    for r in range(4):
        for p in range(2):
            waiting.append((max(LINE_US[r], 0.0), r, p, 1))
    free, times = 0.0, []
    while waiting:
        waiting.sort()
        ready, r, p, d = waiting.pop(0)
        free = max(free, ready) + part_us
        last = 4 if (p == 0) == (sign > 0) else 3
        times.append((free + delay_us + (0.01 if sign < 0 else 0.0), r, p, d, last))
        if d < last:
            waiting.append((free + delay_us, r, p, d + 1))
    return times


def per_device(tokens, norm_gain, in_weight, short_weight, filters):
    weight = jnp.transpose(in_weight, (1, 0, 2))
    vmem = pl.BlockSpec(memory_space=pltpu.VMEM)
    hbm = pl.BlockSpec(memory_space=pl.ANY)
    return pl.pallas_call(
        kernel,
        out_shape=jax.ShapeDtypeStruct((ROWS, COLS), BF16),
        in_specs=[hbm, vmem, hbm, vmem, vmem],
        out_specs=vmem,
        scratch_shapes=[
            pltpu.VMEM((PIECES, EXT, COLS), BF16),
            pltpu.VMEM((PIECES // 2, 2 * COLS, 3 * COLS), BF16),
            pltpu.VMEM((PIECES // 2, ROWS, 2 * COLS), BF16),
            pltpu.VMEM((ROWS, 3 * COLS), F32),
            pltpu.VMEM((ROWS, 128), F32),
            pltpu.VMEM((GROUP * TAPS, 2 * TAPS), BF16),
            pltpu.VMEM((ROWS + 16, 3 * COLS), BF16),
            pltpu.VMEM((ROWS + TAPS, COLS), BF16),
            pltpu.VMEM((HALO, COLS), BF16),
            pltpu.VMEM((HALO, COLS), BF16),
            pltpu.SemaphoreType.DMA((4,)),
            pltpu.SemaphoreType.DMA((N_SENDS,)),
            pltpu.SemaphoreType.DMA((2 * PIECES,)),
            pltpu.SemaphoreType.DMA((PIECES,)),
            pltpu.SemaphoreType.DMA((1,)),
        ],
        compiler_params=pltpu.CompilerParams(
            collective_id=0, has_side_effects=True, vmem_limit_bytes=58 * 1024 * 1024
        ),
        cost_estimate=pl.CostEstimate(
            flops=2 * ROWS * 8192 * 768, bytes_accessed=4 * 1024 * 1024, transcendentals=0
        ),
    )(tokens, norm_gain, weight, short_weight, filters)


def solution(mesh):
    placed = (P("ctx", "tp"), P("tp"), P("ctx", None, "tp"), P(None, None, "tp"), P("tp", None))
    return jax.shard_map(
        per_device, mesh=mesh, in_specs=placed, out_specs=P("ctx", "tp"), check_vma=False
    )
```
